32 devices in a mesh: gx: 4 (over x, core), gy: 4 (over z), gz: 2 (over y).
Axes of the slice: x: 2, y: 2, z: 4, core: 2. Of those that a mesh axis runs over, the one named last changes fastest.
Arguments:
- out_grad_values: bfloat16 [256, 28672], P(('gx', 'gy'), 'gz'), may hold values from -6 to 6
- out_grad_scales: bfloat16 [256, 896], P(('gx', 'gy'), 'gz'), may hold values from 0.099609375 to 1
- pre_activation: bfloat16 [256, 28672], P(('gx', 'gy'), 'gz'), may hold values from -8 to 8
- saved_values: bfloat16 [256, 14336], P('gz', ('gx', 'gy')), may hold values from -6 to 6
- saved_scales: bfloat16 [256, 448], P('gz', ('gx', 'gy')), may hold values from 0.19921875 to 2
- up_weight: bfloat16 [14336, 28672], P(('gx', 'gy'), 'gz'), may hold values from -0.046875 to 0.046875
Outputs:
- grad_input: bfloat16 [256, 14336], P('gz', ('gx', 'gy'))
- grad_weight: bfloat16 [14336, 28672], P(('gx', 'gy'), 'gz')
- grad_bias: float32 [28672], P('gz')
The draws below stay inside these ranges and needn't reach their ends.
All inputs are finite; a program needn't handle non-finite values.
Results may differ from the reference program's by a relative error of at most 0.0059.
Values may be sent and summed in bfloat16 or wider, within the bound.
A program may use at most 192 MiB of HBM per device.

```python
import math
import jax
import jax.numpy as jnp
from jax import lax

D = 14336
HID = 28672
QB = 32
TOKENS = 256
N_GZ = 2


def block_levels(own_key, shape, split, smallest, high):
    level, own = 1.0, jax.random.fold_in(own_key, 6)
    for axis_at, blocks in split:
        heights = jnp.exp(jax.random.uniform(jax.random.fold_in(own, axis_at), (blocks,), jnp.float32, smallest / len(split), high / len(split)))
        level = level * jnp.repeat(heights, shape[axis_at] // blocks).reshape([-1 if axis == axis_at else 1 for axis in range(len(shape))])
    return level


def gaussian(stream_key, extent, scale, most, cuts=(), kind=jnp.bfloat16):
    gain = block_levels(stream_key, extent, cuts, -0.22, 0.18) if cuts else 1.0
    entries = jax.random.normal(stream_key, extent, jnp.float32) * scale * gain
    return jnp.minimum(jnp.maximum(entries, -most), most).astype(kind)


def setup_inputs(seed: int = 0) -> dict:
    key_of = jax.random.split(jax.random.key(seed), 7)
    out_grad_values = gaussian(key_of[0], (TOKENS, HID), 1.0, 6.0, ((0, 16), (1, 2)))
    out_grad_scales = jnp.clip(jnp.exp(math.log(1.0) - 2.306499 * jax.random.uniform(key_of[1], (TOKENS, HID // QB), jnp.float32) ** block_levels(key_of[1], (TOKENS, HID // QB), ((0, 16), (1, 2)), -0.2, 0.2)), 0.099609375, 1.0).astype(jnp.bfloat16)
    pre_activation = gaussian(key_of[2], (TOKENS, HID), 1.5, 8.0, ((0, 16), (1, 2)))
    saved_values = gaussian(key_of[3], (TOKENS, D), 1.0, 6.0, ((0, 2), (1, 16)))
    saved_scales = jnp.clip(jnp.exp(math.log(2.0) - 2.306499 * jax.random.uniform(key_of[4], (TOKENS, D // QB), jnp.float32) ** block_levels(key_of[4], (TOKENS, D // QB), ((0, 2), (1, 16)), -0.2, 0.2)), 0.19921875, 2.0).astype(jnp.bfloat16)
    up_weight = gaussian(key_of[5], (D, HID), D ** -0.5, 0.046875, ((0, 16), (1, 2)))
    return dict(out_grad_values=out_grad_values, out_grad_scales=out_grad_scales, pre_activation=pre_activation, saved_values=saved_values, saved_scales=saved_scales, up_weight=up_weight)


def gelu_slope(preact):
    inner = jnp.tanh(0.79788456 * preact * (1.0 + 0.044715 * preact * preact))
    return 0.5 * preact * ((1.0 - inner * inner) * (0.79788456 + 0.1070322243 * preact * preact)) + 0.5 * (1.0 + inner)


def dequantize(values, scales):
    height = values.shape[0]
    blocks = scales.shape[1]
    shaped = values.astype(jnp.float32).reshape(height, blocks, -1) * scales.astype(jnp.float32)[:, :, None]
    return shaped.reshape(height, -1)


def reference(out_grad_values, out_grad_scales, pre_activation, saved_values, saved_scales, up_weight):
    gradient = dequantize(out_grad_values, out_grad_scales)
    hidden_grad = (gradient * gelu_slope(pre_activation.astype(jnp.float32))).astype(jnp.bfloat16)
    restored = dequantize(saved_values, saved_scales).astype(jnp.bfloat16)
    width = HID // N_GZ
    grad_blocks = jnp.transpose(hidden_grad.reshape(TOKENS, N_GZ, width), (1, 0, 2))
    weight_blocks = jnp.transpose(up_weight.reshape(D, N_GZ, width), (1, 0, 2))

    def one_partial(pair):
        grad_piece, weight_piece = pair
        term = lax.dot_general(grad_piece, weight_piece, (((1,), (1,)), ((), ())), preferred_element_type=jnp.float32)
        return term.astype(jnp.bfloat16)

    partials = lax.map(one_partial, (grad_blocks, weight_blocks))
    grad_input = jnp.sum(partials.astype(jnp.float32), axis=0).astype(jnp.bfloat16)
    grad_weight = lax.dot_general(restored, hidden_grad, (((0,), (0,)), ((), ())), preferred_element_type=jnp.float32).astype(jnp.bfloat16)
    grad_bias = jnp.sum(hidden_grad, axis=0, dtype=jnp.float32)
    return grad_input, grad_weight, grad_bias
```

```python
import functools
import jax
import jax.numpy as jnp
from jax import lax
from jax.experimental import pallas as pl
from jax.experimental.pallas import tpu as pltpu
from jax.sharding import PartitionSpec as P

MESH = pl.DeviceIdType.MESH
WIDTH = 1024
SPAN = 4096


def gelu_slope(preact):
    inner = jnp.tanh(0.79788456 * preact * (1.0 + 0.044715 * preact * preact))
    return 0.5 * preact * (
        (1.0 - inner * inner) * (0.79788456 + 0.1070322243 * preact * preact)
    ) + 0.5 * (1.0 + inner)


def dequantize(values, scales):
    height = values.shape[0]
    blocks = scales.shape[1]
    shaped = (
        values.astype(jnp.float32).reshape(height, blocks, -1)
        * scales.astype(jnp.float32)[:, :, None]
    )
    return shaped.reshape(height, -1)


def slope_product(values, scales, preact):
    return (dequantize(values, scales) * gelu_slope(preact.astype(jnp.float32))).astype(
        jnp.bfloat16
    )


def plain_body(out_grad_values, out_grad_scales, pre_activation, saved_values, saved_scales, up_weight):
    restored = dequantize(saved_values, saved_scales).astype(jnp.bfloat16)
    saved_all = lax.all_gather(restored, "gz", axis=0, tiled=True)
    own_slope = slope_product(out_grad_values, out_grad_scales, pre_activation)
    slope_all = lax.all_gather(own_slope, ("gx", "gy"), axis=0, tiled=True)
    weight_acc = lax.dot_general(
        saved_all, slope_all, (((0,), (0,)), ((), ())), preferred_element_type=jnp.float32
    )
    grad_weight = weight_acc.astype(jnp.bfloat16)
    grad_bias = jnp.sum(slope_all, axis=0, dtype=jnp.float32)
    grad_input = lax.psum_scatter(
        lax.dot_general(
            slope_all, up_weight, (((1,), (1,)), ((), ())), preferred_element_type=jnp.float32
        ).astype(jnp.bfloat16),
        "gz",
        scatter_dimension=0,
        tiled=True,
    )
    return (grad_input, grad_weight, grad_bias)


def gather_kernel(
    nz, values, scales, preact, saved, saved_scales, weight,
    keep, give, bias, saved_t, hid_out,
    hid, wbuf, spread, padded, saved_all, acc,
    w_sem, out_sem, y_send, y_recv,
    right_send, left_send, x_send, sib_send, z_recv, x_recv, sib_recv,
):
    rows = values.shape[0]
    chunks = hid.shape[0]
    width = hid.shape[2]
    per = SPAN // width
    column = nz * rows
    gx, z, y = lax.axis_index("gx"), lax.axis_index("gy"), lax.axis_index("gz")
    x, c = gx // 2, gx % 2
    partner_gx, sib_gx = (1 - x) * 2 + c, x * 2 + 1 - c

    to_right = {"gy": jnp.minimum(z + 1, nz - 1)}
    to_left = {"gy": jnp.maximum(z - 1, 0)}
    to_x, to_sib, to_y = {"gx": partner_gx}, {"gx": sib_gx}, {"gz": 1 - y}

    def block(k, gx_at, z_at):
        at = pl.multiple_of((gx_at * nz + z_at) * rows, rows)
        return hid.at[k, pl.ds(at, rows), :]

    def block_column(k, gx_at):
        return hid.at[k, pl.ds(pl.multiple_of(gx_at * column, column), column), :]

    def landed(ref, sem):
        pltpu.make_async_copy(ref, ref, sem).wait()

    def send(ref, s_sem, r_sem, to):
        pltpu.make_async_remote_copy(
            src_ref=ref, dst_ref=ref, send_sem=s_sem, recv_sem=r_sem,
            device_id=to, device_id_type=MESH,
        ).start()

    def w_copy(k):
        return pltpu.make_async_copy(
            weight.at[:, pl.ds(pl.multiple_of(k * width, width), width)],
            wbuf.at[k], w_sem.at[k],
        )

    barrier = pltpu.get_barrier_semaphore()

    @pl.when(z + 1 < nz)
    def _():
        pl.semaphore_signal(barrier, inc=1, device_id=to_right, device_id_type=MESH)

    @pl.when(z > 0)
    def _():
        pl.semaphore_signal(barrier, inc=1, device_id=to_left, device_id_type=MESH)

    for to in (to_x, to_sib, to_y):
        pl.semaphore_signal(barrier, inc=1, device_id=to, device_id_type=MESH)

    def fetch(k, carry):
        w_copy(k).start()
        return carry

    lax.fori_loop(0, chunks, fetch, 0)

    shape = (128, SPAN)
    spread[...] = (
        lax.broadcasted_iota(jnp.int32, shape, 0)
        == lax.broadcasted_iota(jnp.int32, shape, 1) // 32
    ).astype(jnp.float32).astype(jnp.bfloat16)
    padded[...] = jnp.zeros_like(padded)
    padded[:, : scales.shape[1]] = scales[...]
    acc[...] = jnp.zeros_like(acc)

    middle = jnp.where(z > 0, 1, 0) + jnp.where(z + 1 < nz, 1, 0)
    pl.semaphore_wait(barrier, 3 + middle)

    def own(k):
        cols = pl.ds(pl.multiple_of(k * width, width), width)
        scale = jnp.dot(
            padded[:, pl.ds(pl.multiple_of(k // per * 128, 128), 128)],
            spread[:, pl.ds(pl.multiple_of(k % per * width, width), width)],
            preferred_element_type=jnp.float32,
        )
        gradient = values[:, cols].astype(jnp.float32) * scale
        result = gradient * gelu_slope(preact[:, cols].astype(jnp.float32))
        at = pl.multiple_of((gx * nz + z) * rows, rows)
        hid[k, pl.ds(at, rows), :] = result.astype(jnp.bfloat16)
        forward(k, z, 0, True, True)

    def forward(k, z_at, hop, rightward, leftward):
        ref = block(k, gx, z_at)
        if hop < nz - 1:
            if rightward:
                @pl.when(z + 1 < nz)
                def _():
                    send(ref, right_send.at[hop], z_recv.at[k, z_at], to_right)
            if leftward:
                @pl.when(z > 0)
                def _():
                    send(ref, left_send.at[hop], z_recv.at[k, z_at], to_left)
        send(ref, x_send, x_recv.at[k], to_x)

    def arrived(k, hop):
        @pl.when(z >= hop)
        def _():
            landed(block(k, gx, z - hop), z_recv.at[k, z - hop])
            forward(k, z - hop, hop, True, False)

        @pl.when(z + hop < nz)
        def _():
            landed(block(k, gx, z + hop), z_recv.at[k, z + hop])
            forward(k, z + hop, hop, False, True)

    def from_x(k):
        ref = block_column(k, partner_gx)
        landed(ref, x_recv.at[k])
        send(ref, sib_send, sib_recv.at[k, 1], to_sib)

    def use(k):
        landed(block_column(k, sib_gx), sib_recv.at[k, 0])
        landed(block_column(k, (1 - x) * 2 + 1 - c), sib_recv.at[k, 1])
        pltpu.make_async_copy(hid.at[k], hid_out.at[k], out_sem).start()
        w_copy(k).wait()
        acc[...] += lax.dot_general(
            hid[k], wbuf[k], (((1,), (1,)), ((), ())), preferred_element_type=jnp.float32
        )
        cols = pl.ds(pl.multiple_of(k * width, width), width)
        bias[:, cols] = jnp.sum(hid[k].astype(jnp.float32), axis=0, keepdims=True)

    def within(k, fn):
        @pl.when((k >= 0) & (k < chunks))
        def _():
            fn(k)

    def step(t, carry):
        within(t, own)
        for hop in range(1, nz):
            within(t - hop, functools.partial(arrived, hop=hop))
        within(
            t - (nz - 1),
            lambda k: send(block_column(k, gx), sib_send, sib_recv.at[k, 0], to_sib),
        )
        within(t - nz, from_x)
        within(t - nz - 1, use)
        return carry

    own(0)
    half = saved.shape[0]
    wide = saved.shape[1]
    acc[0:half, 0:128] = jnp.zeros((half, 128), jnp.float32)
    acc[0:half, 0 : saved_scales.shape[1]] = saved_scales[...].astype(jnp.float32)
    restored = (
        jnp.dot(
            acc[0:half, 0:128].astype(jnp.bfloat16), spread[:, :wide],
            preferred_element_type=jnp.float32,
        )
        * saved[...].astype(jnp.float32)
    ).astype(jnp.bfloat16)
    acc[0:half, 0:128] = jnp.zeros((half, 128), jnp.float32)
    own_half = pl.ds(pl.multiple_of(y * half, half), half)
    other_half = pl.ds(pl.multiple_of((1 - y) * half, half), half)
    saved_all[own_half, :] = restored
    send(saved_all.at[own_half, :], y_send, y_recv, to_y)

    lax.fori_loop(1, nz, step, 0)
    lax.fori_loop(nz, chunks, step, 0)
    landed(saved_all.at[other_half, :], y_recv)
    saved_t[...] = saved_all[...].T
    lax.fori_loop(chunks, chunks + nz + 1, step, 0)

    keep[...] = acc[own_half, :].astype(jnp.bfloat16)
    give[...] = acc[other_half, :].astype(jnp.bfloat16)

    landed(saved_all.at[own_half, :], y_send)
    for hop in range(nz - 1):
        @pl.when((z + 1 < nz) & (z >= hop))
        def _():
            landed(hid.at[:, 0:rows, :], right_send.at[hop])

        @pl.when((z > 0) & (z + hop < nz))
        def _():
            landed(hid.at[:, 0:rows, :], left_send.at[hop])

    landed(hid.at[:, 0:column, :], x_send)
    landed(hid.at[:, 0 : 2 * column, :], sib_send)
    pltpu.make_async_copy(hid, hid_out, out_sem).wait()


def weight_kernel(saved_t, hid, bias, out, bias_out):
    out[...] = jnp.dot(
        saved_t[...], hid[0], preferred_element_type=jnp.float32
    ).astype(out.dtype)
    bias_out[...] = bias[...]


def fast_body(nz, values, scales, preact, saved, saved_scales, weight):
    rows, hidden = values.shape
    wide = weight.shape[0]
    half = saved.shape[0]
    tokens = 4 * nz * rows
    chunks = hidden // WIDTH
    vmem = pl.BlockSpec(memory_space=pltpu.VMEM)
    hbm = pl.BlockSpec(memory_space=pltpu.HBM)
    dma = pltpu.SemaphoreType.DMA
    keep, give, bias, saved_t, hid = pl.pallas_call(
        functools.partial(gather_kernel, nz),
        out_shape=(
            jax.ShapeDtypeStruct((half, wide), jnp.bfloat16),
            jax.ShapeDtypeStruct((half, wide), jnp.bfloat16),
            jax.ShapeDtypeStruct((1, hidden), jnp.float32),
            jax.ShapeDtypeStruct((wide, tokens), jnp.bfloat16),
            jax.ShapeDtypeStruct((chunks, tokens, WIDTH), jnp.bfloat16),
        ),
        in_specs=[vmem] * 5 + [hbm],
        out_specs=(vmem, vmem, vmem, vmem, hbm),
        scratch_shapes=[
            pltpu.VMEM((chunks, tokens, WIDTH), jnp.bfloat16),
            pltpu.VMEM((chunks, wide, WIDTH), jnp.bfloat16),
            pltpu.VMEM((128, SPAN), jnp.bfloat16),
            pltpu.VMEM((rows, pl.cdiv(scales.shape[1], 128) * 128), jnp.bfloat16),
            pltpu.VMEM((tokens, wide), jnp.bfloat16),
            pltpu.VMEM((tokens, wide), jnp.float32),
            dma((chunks,)), dma, dma, dma,
            dma((nz - 1,)), dma((nz - 1,)), dma, dma,
            dma((chunks, nz)), dma((chunks,)), dma((chunks, 2)),
        ],
        compiler_params=pltpu.CompilerParams(
            collective_id=0, has_side_effects=True, vmem_limit_bytes=52 << 20
        ),
        cost_estimate=pl.CostEstimate(
            flops=2 * tokens * hidden * wide,
            bytes_accessed=2 * hidden * (wide + tokens),
            transcendentals=rows * hidden,
        ),
        name="gather",
    )(values, scales, preact, saved, saved_scales, weight)
    taken = lax.ppermute(give, "gz", [(0, 1), (1, 0)])
    grad_weight, grad_bias = pl.pallas_call(
        weight_kernel,
        grid=(chunks,),
        out_shape=(
            jax.ShapeDtypeStruct((wide, hidden), jnp.bfloat16),
            jax.ShapeDtypeStruct((1, hidden), jnp.float32),
        ),
        in_specs=[
            pl.BlockSpec((wide, tokens), lambda i: (0, 0)),
            pl.BlockSpec((1, tokens, WIDTH), lambda i: (i, 0, 0)),
            pl.BlockSpec((1, WIDTH), lambda i: (0, i)),
        ],
        out_specs=(
            pl.BlockSpec((wide, WIDTH), lambda i: (0, i)),
            pl.BlockSpec((1, WIDTH), lambda i: (0, i)),
        ),
        compiler_params=pltpu.CompilerParams(vmem_limit_bytes=32 << 20),
        cost_estimate=pl.CostEstimate(
            flops=2 * tokens * hidden * wide,
            bytes_accessed=2 * hidden * (wide + tokens),
            transcendentals=0,
        ),
        name="weight",
    )(saved_t, hid, bias)
    grad_input = (keep.astype(jnp.float32) + taken.astype(jnp.float32)).astype(jnp.bfloat16)
    return grad_input, grad_weight, grad_bias.reshape(-1)


def solution(mesh):
    placed = (
        P(("gx", "gy"), "gz"),
        P(("gx", "gy"), "gz"),
        P(("gx", "gy"), "gz"),
        P("gz", ("gx", "gy")),
        P("gz", ("gx", "gy")),
        P(("gx", "gy"), "gz"),
    )
    body = plain_body
    if mesh.shape["gx"] == 4 and mesh.shape["gz"] == 2:
        body = functools.partial(fast_body, mesh.shape["gy"])
    return jax.shard_map(
        body,
        mesh=mesh,
        in_specs=placed,
        out_specs=(P("gz", ("gx", "gy")), P(("gx", "gy"), "gz"), P("gz")),
        check_vma=False,
    )
```

```python
import functools
import jax
import jax.numpy as jnp
from jax import lax
from jax.experimental import pallas as pl
from jax.experimental.pallas import tpu as pltpu
from jax.sharding import PartitionSpec as P

MESH = pl.DeviceIdType.MESH
WIDTH = 1024
PAIR = 2
SPAN = 4096


def gelu_slope(preact):
    inner = jnp.tanh(0.79788456 * preact * (1.0 + 0.044715 * preact * preact))
    return 0.5 * preact * (
        (1.0 - inner * inner) * (0.79788456 + 0.1070322243 * preact * preact)
    ) + 0.5 * (1.0 + inner)


def dequantize(values, scales):
    height = values.shape[0]
    blocks = scales.shape[1]
    shaped = (
        values.astype(jnp.float32).reshape(height, blocks, -1)
        * scales.astype(jnp.float32)[:, :, None]
    )
    return shaped.reshape(height, -1)


def slope_product(values, scales, preact):
    return (dequantize(values, scales) * gelu_slope(preact.astype(jnp.float32))).astype(
        jnp.bfloat16
    )


def plain_body(out_grad_values, out_grad_scales, pre_activation, saved_values, saved_scales, up_weight):
    restored = dequantize(saved_values, saved_scales).astype(jnp.bfloat16)
    saved_all = lax.all_gather(restored, "gz", axis=0, tiled=True)
    own_slope = slope_product(out_grad_values, out_grad_scales, pre_activation)
    slope_all = lax.all_gather(own_slope, ("gx", "gy"), axis=0, tiled=True)
    weight_acc = lax.dot_general(
        saved_all, slope_all, (((0,), (0,)), ((), ())), preferred_element_type=jnp.float32
    )
    grad_weight = weight_acc.astype(jnp.bfloat16)
    grad_bias = jnp.sum(slope_all, axis=0, dtype=jnp.float32)
    grad_input = lax.psum_scatter(
        lax.dot_general(
            slope_all, up_weight, (((1,), (1,)), ((), ())), preferred_element_type=jnp.float32
        ).astype(jnp.bfloat16),
        "gz",
        scatter_dimension=0,
        tiled=True,
    )
    return (grad_input, grad_weight, grad_bias)


def gather_kernel(
    nz, values, scales, preact, saved, saved_scales, weight,
    keep, give, bias, saved_t, hid_out,
    hid, wbuf, spread, padded, saved_all, acc,
    w_sem, out_sem, y_send, y_recv,
    right_send, left_send, x_send, sib_send, z_recv, x_recv, sib_recv,
):
    rows = values.shape[0]
    chunks = hid.shape[0]
    width = hid.shape[2]
    per = SPAN // width
    column = nz * rows
    gx, z, y = lax.axis_index("gx"), lax.axis_index("gy"), lax.axis_index("gz")
    x, c = gx // 2, gx % 2
    partner_gx, sib_gx = (1 - x) * 2 + c, x * 2 + 1 - c

    to_right = {"gy": jnp.minimum(z + 1, nz - 1)}
    to_left = {"gy": jnp.maximum(z - 1, 0)}
    to_x, to_sib, to_y = {"gx": partner_gx}, {"gx": sib_gx}, {"gz": 1 - y}

    def block(k, gx_at, z_at):
        at = pl.multiple_of((gx_at * nz + z_at) * rows, rows)
        return hid.at[k, pl.ds(at, rows), :]

    def block_column(k, gx_at):
        return hid.at[k, pl.ds(pl.multiple_of(gx_at * column, column), column), :]

    def landed(ref, sem):
        pltpu.make_async_copy(ref, ref, sem).wait()

    def send(ref, s_sem, r_sem, to):
        pltpu.make_async_remote_copy(
            src_ref=ref, dst_ref=ref, send_sem=s_sem, recv_sem=r_sem,
            device_id=to, device_id_type=MESH,
        ).start()

    def w_copy(k):
        return pltpu.make_async_copy(
            weight.at[:, pl.ds(pl.multiple_of(k * width, width), width)],
            wbuf.at[k], w_sem.at[k],
        )

    barrier = pltpu.get_barrier_semaphore()

    @pl.when(z + 1 < nz)
    def _():
        pl.semaphore_signal(barrier, inc=1, device_id=to_right, device_id_type=MESH)

    @pl.when(z > 0)
    def _():
        pl.semaphore_signal(barrier, inc=1, device_id=to_left, device_id_type=MESH)

    for to in (to_x, to_sib, to_y):
        pl.semaphore_signal(barrier, inc=1, device_id=to, device_id_type=MESH)

    def fetch(k, carry):
        w_copy(k).start()
        return carry

    lax.fori_loop(0, chunks, fetch, 0)

    shape = (128, SPAN)
    spread[...] = (
        lax.broadcasted_iota(jnp.int32, shape, 0)
        == lax.broadcasted_iota(jnp.int32, shape, 1) // 32
    ).astype(jnp.float32).astype(jnp.bfloat16)
    padded[...] = jnp.zeros_like(padded)
    padded[:, : scales.shape[1]] = scales[...]
    acc[...] = jnp.zeros_like(acc)

    middle = jnp.where(z > 0, 1, 0) + jnp.where(z + 1 < nz, 1, 0)
    pl.semaphore_wait(barrier, 3 + middle)

    def own(k):
        cols = pl.ds(pl.multiple_of(k * width, width), width)
        scale = jnp.dot(
            padded[:, pl.ds(pl.multiple_of(k // per * 128, 128), 128)],
            spread[:, pl.ds(pl.multiple_of(k % per * width, width), width)],
            preferred_element_type=jnp.float32,
        )
        gradient = values[:, cols].astype(jnp.float32) * scale
        result = gradient * gelu_slope(preact[:, cols].astype(jnp.float32))
        at = pl.multiple_of((gx * nz + z) * rows, rows)
        hid[k, pl.ds(at, rows), :] = result.astype(jnp.bfloat16)
        forward(k, z, 0, True, True)

    def forward(k, z_at, hop, rightward, leftward):
        ref = block(k, gx, z_at)
        if hop < nz - 1:
            if rightward:
                @pl.when(z + 1 < nz)
                def _():
                    send(ref, right_send.at[hop], z_recv.at[k, z_at], to_right)
            if leftward:
                @pl.when(z > 0)
                def _():
                    send(ref, left_send.at[hop], z_recv.at[k, z_at], to_left)
        send(ref, x_send, x_recv.at[k], to_x)

    def arrived(k, hop):
        @pl.when(z >= hop)
        def _():
            landed(block(k, gx, z - hop), z_recv.at[k, z - hop])
            forward(k, z - hop, hop, True, False)

        @pl.when(z + hop < nz)
        def _():
            landed(block(k, gx, z + hop), z_recv.at[k, z + hop])
            forward(k, z + hop, hop, False, True)

    def from_x(k):
        ref = block_column(k, partner_gx)
        landed(ref, x_recv.at[k])
        send(ref, sib_send, sib_recv.at[k, 1], to_sib)

    def use(k):
        landed(block_column(k, sib_gx), sib_recv.at[k, 0])
        landed(block_column(k, (1 - x) * 2 + 1 - c), sib_recv.at[k, 1])
        pltpu.make_async_copy(hid.at[k], hid_out.at[k], out_sem).start()
        w_copy(k).wait()
        acc[...] += lax.dot_general(
            hid[k], wbuf[k], (((1,), (1,)), ((), ())), preferred_element_type=jnp.float32
        )
        cols = pl.ds(pl.multiple_of(k * width, width), width)
        bias[:, cols] = jnp.sum(hid[k].astype(jnp.float32), axis=0, keepdims=True)

    def within(k, fn):
        @pl.when((k >= 0) & (k < chunks))
        def _():
            fn(k)

    def step(t, carry):
        within(t, own)
        for hop in range(1, nz):
            within(t - hop, functools.partial(arrived, hop=hop))
        within(
            t - (nz - 1),
            lambda k: send(block_column(k, gx), sib_send, sib_recv.at[k, 0], to_sib),
        )
        within(t - nz, from_x)
        within(t - nz - 1, use)
        return carry

    own(0)
    half = saved.shape[0]
    wide = saved.shape[1]
    acc[0:half, 0:128] = jnp.zeros((half, 128), jnp.float32)
    acc[0:half, 0 : saved_scales.shape[1]] = saved_scales[...].astype(jnp.float32)
    restored = (
        jnp.dot(
            acc[0:half, 0:128].astype(jnp.bfloat16), spread[:, :wide],
            preferred_element_type=jnp.float32,
        )
        * saved[...].astype(jnp.float32)
    ).astype(jnp.bfloat16)
    acc[0:half, 0:128] = jnp.zeros((half, 128), jnp.float32)
    own_half = pl.ds(pl.multiple_of(y * half, half), half)
    other_half = pl.ds(pl.multiple_of((1 - y) * half, half), half)
    saved_all[own_half, :] = restored
    send(saved_all.at[own_half, :], y_send, y_recv, to_y)

    lax.fori_loop(1, nz, step, 0)
    lax.fori_loop(nz, chunks, step, 0)
    landed(saved_all.at[other_half, :], y_recv)
    saved_t[...] = saved_all[...].T
    lax.fori_loop(chunks, chunks + nz + 1, step, 0)

    keep[...] = acc[own_half, :].astype(jnp.bfloat16)
    give[...] = acc[other_half, :].astype(jnp.bfloat16)

    landed(saved_all.at[own_half, :], y_send)
    for hop in range(nz - 1):
        @pl.when((z + 1 < nz) & (z >= hop))
        def _():
            landed(hid.at[:, 0:rows, :], right_send.at[hop])

        @pl.when((z > 0) & (z + hop < nz))
        def _():
            landed(hid.at[:, 0:rows, :], left_send.at[hop])

    landed(hid.at[:, 0:column, :], x_send)
    landed(hid.at[:, 0 : 2 * column, :], sib_send)
    pltpu.make_async_copy(hid, hid_out, out_sem).wait()


def weight_kernel(saved_t, hid, bias, out, bias_out):
    for i in range(PAIR):
        out[:, i * WIDTH : (i + 1) * WIDTH] = jnp.dot(
            saved_t[...], hid[i], preferred_element_type=jnp.float32
        ).astype(out.dtype)
    bias_out[...] = bias[...]


def fast_body(nz, values, scales, preact, saved, saved_scales, weight):
    rows, hidden = values.shape
    wide = weight.shape[0]
    half = saved.shape[0]
    tokens = 4 * nz * rows
    chunks = hidden // WIDTH
    vmem = pl.BlockSpec(memory_space=pltpu.VMEM)
    hbm = pl.BlockSpec(memory_space=pltpu.HBM)
    dma = pltpu.SemaphoreType.DMA
    keep, give, bias, saved_t, hid = pl.pallas_call(
        functools.partial(gather_kernel, nz),
        out_shape=(
            jax.ShapeDtypeStruct((half, wide), jnp.bfloat16),
            jax.ShapeDtypeStruct((half, wide), jnp.bfloat16),
            jax.ShapeDtypeStruct((1, hidden), jnp.float32),
            jax.ShapeDtypeStruct((wide, tokens), jnp.bfloat16),
            jax.ShapeDtypeStruct((chunks, tokens, WIDTH), jnp.bfloat16),
        ),
        in_specs=[vmem] * 5 + [hbm],
        out_specs=(vmem, vmem, vmem, vmem, hbm),
        scratch_shapes=[
            pltpu.VMEM((chunks, tokens, WIDTH), jnp.bfloat16),
            pltpu.VMEM((chunks, wide, WIDTH), jnp.bfloat16),
            pltpu.VMEM((128, SPAN), jnp.bfloat16),
            pltpu.VMEM((rows, pl.cdiv(scales.shape[1], 128) * 128), jnp.bfloat16),
            pltpu.VMEM((tokens, wide), jnp.bfloat16),
            pltpu.VMEM((tokens, wide), jnp.float32),
            dma((chunks,)), dma, dma, dma,
            dma((nz - 1,)), dma((nz - 1,)), dma, dma,
            dma((chunks, nz)), dma((chunks,)), dma((chunks, 2)),
        ],
        compiler_params=pltpu.CompilerParams(
            collective_id=0, has_side_effects=True, vmem_limit_bytes=52 << 20
        ),
        cost_estimate=pl.CostEstimate(
            flops=2 * tokens * hidden * wide,
            bytes_accessed=2 * hidden * (wide + tokens),
            transcendentals=rows * hidden,
        ),
        name="gather",
    )(values, scales, preact, saved, saved_scales, weight)
    taken = lax.ppermute(give, "gz", [(0, 1), (1, 0)])
    grad_weight, grad_bias = pl.pallas_call(
        weight_kernel,
        grid=(chunks // PAIR,),
        out_shape=(
            jax.ShapeDtypeStruct((wide, hidden), jnp.bfloat16),
            jax.ShapeDtypeStruct((1, hidden), jnp.float32),
        ),
        in_specs=[
            pl.BlockSpec((wide, tokens), lambda i: (0, 0)),
            pl.BlockSpec((PAIR, tokens, WIDTH), lambda i: (i, 0, 0)),
            pl.BlockSpec((1, PAIR * WIDTH), lambda i: (0, i)),
        ],
        out_specs=(
            pl.BlockSpec((wide, PAIR * WIDTH), lambda i: (0, i)),
            pl.BlockSpec((1, PAIR * WIDTH), lambda i: (0, i)),
        ),
        compiler_params=pltpu.CompilerParams(vmem_limit_bytes=32 << 20),
        cost_estimate=pl.CostEstimate(
            flops=2 * tokens * hidden * wide,
            bytes_accessed=2 * hidden * (wide + tokens),
            transcendentals=0,
        ),
        name="weight",
    )(saved_t, hid, bias)
    grad_input = (keep.astype(jnp.float32) + taken.astype(jnp.float32)).astype(jnp.bfloat16)
    return grad_input, grad_weight, grad_bias.reshape(-1)


def solution(mesh):
    placed = (
        P(("gx", "gy"), "gz"),
        P(("gx", "gy"), "gz"),
        P(("gx", "gy"), "gz"),
        P("gz", ("gx", "gy")),
        P("gz", ("gx", "gy")),
        P(("gx", "gy"), "gz"),
    )
    body = plain_body
    if mesh.shape["gx"] == 4 and mesh.shape["gz"] == 2:
        body = functools.partial(fast_body, mesh.shape["gy"])
    return jax.shard_map(
        body,
        mesh=mesh,
        in_specs=placed,
        out_specs=(P("gz", ("gx", "gy")), P(("gx", "gy"), "gz"), P("gz")),
        check_vma=False,
    )
```

```python
import functools
import jax
import jax.numpy as jnp
from jax import lax
from jax.experimental import pallas as pl
from jax.experimental.pallas import tpu as pltpu
from jax.sharding import PartitionSpec as P

MESH = pl.DeviceIdType.MESH
WIDTH = 2048
PAIR = 1
SPAN = 4096


def gelu_slope(preact):
    inner = jnp.tanh(0.79788456 * preact * (1.0 + 0.044715 * preact * preact))
    return 0.5 * preact * (
        (1.0 - inner * inner) * (0.79788456 + 0.1070322243 * preact * preact)
    ) + 0.5 * (1.0 + inner)


def dequantize(values, scales):
    height = values.shape[0]
    blocks = scales.shape[1]
    shaped = (
        values.astype(jnp.float32).reshape(height, blocks, -1)
        * scales.astype(jnp.float32)[:, :, None]
    )
    return shaped.reshape(height, -1)


def slope_product(values, scales, preact):
    return (dequantize(values, scales) * gelu_slope(preact.astype(jnp.float32))).astype(
        jnp.bfloat16
    )


def plain_body(out_grad_values, out_grad_scales, pre_activation, saved_values, saved_scales, up_weight):
    restored = dequantize(saved_values, saved_scales).astype(jnp.bfloat16)
    saved_all = lax.all_gather(restored, "gz", axis=0, tiled=True)
    own_slope = slope_product(out_grad_values, out_grad_scales, pre_activation)
    slope_all = lax.all_gather(own_slope, ("gx", "gy"), axis=0, tiled=True)
    weight_acc = lax.dot_general(
        saved_all, slope_all, (((0,), (0,)), ((), ())), preferred_element_type=jnp.float32
    )
    grad_weight = weight_acc.astype(jnp.bfloat16)
    grad_bias = jnp.sum(slope_all, axis=0, dtype=jnp.float32)
    grad_input = lax.psum_scatter(
        lax.dot_general(
            slope_all, up_weight, (((1,), (1,)), ((), ())), preferred_element_type=jnp.float32
        ).astype(jnp.bfloat16),
        "gz",
        scatter_dimension=0,
        tiled=True,
    )
    return (grad_input, grad_weight, grad_bias)


def gather_kernel(
    nz, values, scales, preact, saved, saved_scales, weight,
    keep, give, bias, saved_t, hid_out,
    hid, wbuf, spread, padded, saved_all, acc,
    w_sem, out_sem, y_send, y_recv,
    right_send, left_send, x_send, sib_send, z_recv, x_recv, sib_recv,
):
    rows = values.shape[0]
    chunks = hid.shape[0]
    width = hid.shape[2]
    per = SPAN // width
    column = nz * rows
    gx, z, y = lax.axis_index("gx"), lax.axis_index("gy"), lax.axis_index("gz")
    x, c = gx // 2, gx % 2
    partner_gx, sib_gx = (1 - x) * 2 + c, x * 2 + 1 - c

    to_right = {"gy": jnp.minimum(z + 1, nz - 1)}
    to_left = {"gy": jnp.maximum(z - 1, 0)}
    to_x, to_sib, to_y = {"gx": partner_gx}, {"gx": sib_gx}, {"gz": 1 - y}

    def block(k, gx_at, z_at):
        at = pl.multiple_of((gx_at * nz + z_at) * rows, rows)
        return hid.at[k, pl.ds(at, rows), :]

    def block_column(k, gx_at):
        return hid.at[k, pl.ds(pl.multiple_of(gx_at * column, column), column), :]

    def landed(ref, sem):
        pltpu.make_async_copy(ref, ref, sem).wait()

    def send(ref, s_sem, r_sem, to):
        pltpu.make_async_remote_copy(
            src_ref=ref, dst_ref=ref, send_sem=s_sem, recv_sem=r_sem,
            device_id=to, device_id_type=MESH,
        ).start()

    def w_copy(k):
        return pltpu.make_async_copy(
            weight.at[:, pl.ds(pl.multiple_of(k * width, width), width)],
            wbuf.at[k], w_sem.at[k],
        )

    barrier = pltpu.get_barrier_semaphore()

    @pl.when(z + 1 < nz)
    def _():
        pl.semaphore_signal(barrier, inc=1, device_id=to_right, device_id_type=MESH)

    @pl.when(z > 0)
    def _():
        pl.semaphore_signal(barrier, inc=1, device_id=to_left, device_id_type=MESH)

    for to in (to_x, to_sib, to_y):
        pl.semaphore_signal(barrier, inc=1, device_id=to, device_id_type=MESH)

    def fetch(k, carry):
        w_copy(k).start()
        return carry

    lax.fori_loop(0, chunks, fetch, 0)

    shape = (128, SPAN)
    spread[...] = (
        lax.broadcasted_iota(jnp.int32, shape, 0)
        == lax.broadcasted_iota(jnp.int32, shape, 1) // 32
    ).astype(jnp.float32).astype(jnp.bfloat16)
    padded[...] = jnp.zeros_like(padded)
    padded[:, : scales.shape[1]] = scales[...]
    acc[...] = jnp.zeros_like(acc)

    middle = jnp.where(z > 0, 1, 0) + jnp.where(z + 1 < nz, 1, 0)
    pl.semaphore_wait(barrier, 3 + middle)

    def own(k):
        cols = pl.ds(pl.multiple_of(k * width, width), width)
        scale = jnp.dot(
            padded[:, pl.ds(pl.multiple_of(k // per * 128, 128), 128)],
            spread[:, pl.ds(pl.multiple_of(k % per * width, width), width)],
            preferred_element_type=jnp.float32,
        )
        gradient = values[:, cols].astype(jnp.float32) * scale
        result = gradient * gelu_slope(preact[:, cols].astype(jnp.float32))
        at = pl.multiple_of((gx * nz + z) * rows, rows)
        hid[k, pl.ds(at, rows), :] = result.astype(jnp.bfloat16)
        forward(k, z, 0, True, True)

    def forward(k, z_at, hop, rightward, leftward):
        ref = block(k, gx, z_at)
        if hop < nz - 1:
            if rightward:
                @pl.when(z + 1 < nz)
                def _():
                    send(ref, right_send.at[hop], z_recv.at[k, z_at], to_right)
            if leftward:
                @pl.when(z > 0)
                def _():
                    send(ref, left_send.at[hop], z_recv.at[k, z_at], to_left)
        send(ref, x_send, x_recv.at[k], to_x)

    def arrived(k, hop):
        @pl.when(z >= hop)
        def _():
            landed(block(k, gx, z - hop), z_recv.at[k, z - hop])
            forward(k, z - hop, hop, True, False)

        @pl.when(z + hop < nz)
        def _():
            landed(block(k, gx, z + hop), z_recv.at[k, z + hop])
            forward(k, z + hop, hop, False, True)

    def from_x(k):
        ref = block_column(k, partner_gx)
        landed(ref, x_recv.at[k])
        send(ref, sib_send, sib_recv.at[k, 1], to_sib)

    def use(k):
        landed(block_column(k, sib_gx), sib_recv.at[k, 0])
        landed(block_column(k, (1 - x) * 2 + 1 - c), sib_recv.at[k, 1])
        pltpu.make_async_copy(hid.at[k], hid_out.at[k], out_sem).start()
        w_copy(k).wait()
        acc[...] += lax.dot_general(
            hid[k], wbuf[k], (((1,), (1,)), ((), ())), preferred_element_type=jnp.float32
        )
        cols = pl.ds(pl.multiple_of(k * width, width), width)
        bias[:, cols] = jnp.sum(hid[k].astype(jnp.float32), axis=0, keepdims=True)

    def within(k, fn):
        @pl.when((k >= 0) & (k < chunks))
        def _():
            fn(k)

    def step(t, carry):
        within(t, own)
        for hop in range(1, nz):
            within(t - hop, functools.partial(arrived, hop=hop))
        within(
            t - (nz - 1),
            lambda k: send(block_column(k, gx), sib_send, sib_recv.at[k, 0], to_sib),
        )
        within(t - nz, from_x)
        within(t - nz - 1, use)
        return carry

    own(0)
    half = saved.shape[0]
    wide = saved.shape[1]
    acc[0:half, 0:128] = jnp.zeros((half, 128), jnp.float32)
    acc[0:half, 0 : saved_scales.shape[1]] = saved_scales[...].astype(jnp.float32)
    restored = (
        jnp.dot(
            acc[0:half, 0:128].astype(jnp.bfloat16), spread[:, :wide],
            preferred_element_type=jnp.float32,
        )
        * saved[...].astype(jnp.float32)
    ).astype(jnp.bfloat16)
    acc[0:half, 0:128] = jnp.zeros((half, 128), jnp.float32)
    own_half = pl.ds(pl.multiple_of(y * half, half), half)
    other_half = pl.ds(pl.multiple_of((1 - y) * half, half), half)
    saved_all[own_half, :] = restored
    send(saved_all.at[own_half, :], y_send, y_recv, to_y)

    lax.fori_loop(1, nz, step, 0)
    lax.fori_loop(nz, chunks, step, 0)
    landed(saved_all.at[other_half, :], y_recv)
    saved_t[...] = saved_all[...].T
    lax.fori_loop(chunks, chunks + nz + 1, step, 0)

    keep[...] = acc[own_half, :].astype(jnp.bfloat16)
    give[...] = acc[other_half, :].astype(jnp.bfloat16)

    landed(saved_all.at[own_half, :], y_send)
    for hop in range(nz - 1):
        @pl.when((z + 1 < nz) & (z >= hop))
        def _():
            landed(hid.at[:, 0:rows, :], right_send.at[hop])

        @pl.when((z > 0) & (z + hop < nz))
        def _():
            landed(hid.at[:, 0:rows, :], left_send.at[hop])

    landed(hid.at[:, 0:column, :], x_send)
    landed(hid.at[:, 0 : 2 * column, :], sib_send)
    pltpu.make_async_copy(hid, hid_out, out_sem).wait()


def weight_kernel(saved_t, hid, bias, out, bias_out):
    for i in range(PAIR):
        out[:, i * WIDTH : (i + 1) * WIDTH] = jnp.dot(
            saved_t[...], hid[i], preferred_element_type=jnp.float32
        ).astype(out.dtype)
    bias_out[...] = bias[...]


def fast_body(nz, values, scales, preact, saved, saved_scales, weight):
    rows, hidden = values.shape
    wide = weight.shape[0]
    half = saved.shape[0]
    tokens = 4 * nz * rows
    chunks = hidden // WIDTH
    vmem = pl.BlockSpec(memory_space=pltpu.VMEM)
    hbm = pl.BlockSpec(memory_space=pltpu.HBM)
    dma = pltpu.SemaphoreType.DMA
    keep, give, bias, saved_t, hid = pl.pallas_call(
        functools.partial(gather_kernel, nz),
        out_shape=(
            jax.ShapeDtypeStruct((half, wide), jnp.bfloat16),
            jax.ShapeDtypeStruct((half, wide), jnp.bfloat16),
            jax.ShapeDtypeStruct((1, hidden), jnp.float32),
            jax.ShapeDtypeStruct((wide, tokens), jnp.bfloat16),
            jax.ShapeDtypeStruct((chunks, tokens, WIDTH), jnp.bfloat16),
        ),
        in_specs=[vmem] * 5 + [hbm],
        out_specs=(vmem, vmem, vmem, vmem, hbm),
        scratch_shapes=[
            pltpu.VMEM((chunks, tokens, WIDTH), jnp.bfloat16),
            pltpu.VMEM((chunks, wide, WIDTH), jnp.bfloat16),
            pltpu.VMEM((128, SPAN), jnp.bfloat16),
            pltpu.VMEM((rows, pl.cdiv(scales.shape[1], 128) * 128), jnp.bfloat16),
            pltpu.VMEM((tokens, wide), jnp.bfloat16),
            pltpu.VMEM((tokens, wide), jnp.float32),
            dma((chunks,)), dma, dma, dma,
            dma((nz - 1,)), dma((nz - 1,)), dma, dma,
            dma((chunks, nz)), dma((chunks,)), dma((chunks, 2)),
        ],
        compiler_params=pltpu.CompilerParams(
            collective_id=0, has_side_effects=True, vmem_limit_bytes=52 << 20
        ),
        cost_estimate=pl.CostEstimate(
            flops=2 * tokens * hidden * wide,
            bytes_accessed=2 * hidden * (wide + tokens),
            transcendentals=rows * hidden,
        ),
        name="gather",
    )(values, scales, preact, saved, saved_scales, weight)
    taken = lax.ppermute(give, "gz", [(0, 1), (1, 0)])
    grad_weight, grad_bias = pl.pallas_call(
        weight_kernel,
        grid=(chunks // PAIR,),
        out_shape=(
            jax.ShapeDtypeStruct((wide, hidden), jnp.bfloat16),
            jax.ShapeDtypeStruct((1, hidden), jnp.float32),
        ),
        in_specs=[
            pl.BlockSpec((wide, tokens), lambda i: (0, 0)),
            pl.BlockSpec((PAIR, tokens, WIDTH), lambda i: (i, 0, 0)),
            pl.BlockSpec((1, PAIR * WIDTH), lambda i: (0, i)),
        ],
        out_specs=(
            pl.BlockSpec((wide, PAIR * WIDTH), lambda i: (0, i)),
            pl.BlockSpec((1, PAIR * WIDTH), lambda i: (0, i)),
        ),
        compiler_params=pltpu.CompilerParams(vmem_limit_bytes=32 << 20),
        cost_estimate=pl.CostEstimate(
            flops=2 * tokens * hidden * wide,
            bytes_accessed=2 * hidden * (wide + tokens),
            transcendentals=0,
        ),
        name="weight",
    )(saved_t, hid, bias)
    grad_input = (keep.astype(jnp.float32) + taken.astype(jnp.float32)).astype(jnp.bfloat16)
    return grad_input, grad_weight, grad_bias.reshape(-1)


def solution(mesh):
    placed = (
        P(("gx", "gy"), "gz"),
        P(("gx", "gy"), "gz"),
        P(("gx", "gy"), "gz"),
        P("gz", ("gx", "gy")),
        P("gz", ("gx", "gy")),
        P(("gx", "gy"), "gz"),
    )
    body = plain_body
    if mesh.shape["gx"] == 4 and mesh.shape["gz"] == 2:
        body = functools.partial(fast_body, mesh.shape["gy"])
    return jax.shard_map(
        body,
        mesh=mesh,
        in_specs=placed,
        out_specs=(P("gz", ("gx", "gy")), P(("gx", "gy"), "gz"), P("gz")),
        check_vma=False,
    )
```
